32 devices in a mesh: parts: 2 (over y), blk: 4 (over z), sub: 4 (over x, core).
Axes of the slice: x: 2, y: 2, z: 4, core: 2. Of those that a mesh axis runs over, the one named last changes fastest.
Arguments:
- readings: float32 [2, 24576, 256], P(None, ('parts', 'blk', 'sub')), parts along dimension 1, may hold values from -6 to 6
- coverage: int32 [2, 24576, 256], P(None, ('parts', 'blk', 'sub')), parts along dimension 1, may hold values 0 or 1
- pixel_factors: float32 [24576, 256], P(('parts', 'blk', 'sub')), parts along dimension 0, may hold values from -1.5 to 1.5
- date_factors: float32 [2048, 256], P(('parts', 'blk', 'sub')), parts along dimension 0, may hold values from -1.5 to 1.5
Outputs:
- pixel_out: float32 [24576, 256], P(('parts', 'blk', 'sub')), parts along dimension 0
- date_out: float32 [2048, 256], P(('parts', 'blk', 'sub')), parts along dimension 0
The draws below stay inside these ranges and needn't reach their ends.
There are 2 independent parts, one for each index of `parts`. The reference program is written for one: setup_inputs(seed, part) draws one part's arguments, and reference() takes and returns one part's arrays. A program takes and returns all parts, laid end to end along the dimension named above; each array names one. Nothing has to cross between parts.
All inputs are finite; a program needn't handle non-finite values. No bound on the sum of `coverage` on one device may be relied on, other than what follows from the above.
Results may differ from the reference program's by a relative error of at most 0.0001.
Values sent between devices are 32-bit elements; how exact they have to be, the bound alone decides.
A program may use at most 64 MiB of HBM per device.

```python
import jax
import jax.numpy as jnp
from jax import lax

RANK = 256
DB = 256
STRATA = 2
GP = 3072
PIXELS = 12288
DATES = 1024
N_BLK = 4


def set_ends(entries, key, least, largest):
    longest = entries.shape.index(max(entries.shape))
    spots = []
    for shift in (0, 1):
        where = [jax.random.randint(jax.random.fold_in(key, axis), (), 0, length) for axis, length in enumerate(entries.shape)]
        where[longest] = (where[longest] + shift) % entries.shape[longest]
        spots.append(tuple(where))
    return entries.at[spots[0]].set(least).at[spots[1]].set(largest)


def steps_of(rng, dims, split, low, top_value):
    factor_of = 1.0
    for axis_at, shards_of in split:
        steps = jax.random.uniform(jax.random.fold_in(jax.random.fold_in(rng, 6), axis_at), (shards_of,), jnp.float32, low / len(split), top_value / len(split))
        factor_of = factor_of * jnp.repeat(jnp.exp(steps), dims[axis_at] // shards_of).reshape((-1,) + (1,) * (len(dims) - 1 - axis_at))
    return factor_of


def normal_values(key, extent, spread, bound, cuts=(), kind=jnp.bfloat16):
    level = steps_of(key, extent, cuts, -0.22, 0.18) if cuts else 1.0
    entries = jax.random.normal(key, extent, jnp.float32) * spread * level
    return jnp.minimum(jnp.maximum(entries, -bound), bound).astype(kind)


def setup_inputs(seed: int = 0, part: int = 0) -> dict:
    arg_keys = jax.random.split(jax.random.key(seed), 5)
    part_keys = jax.random.split(jax.random.fold_in(arg_keys[4], part), 5)
    readings = normal_values(part_keys[0], (STRATA, PIXELS, DB), 1.0, 6.0, ((1, 16),), jnp.float32)
    coverage = set_ends((jax.random.randint(part_keys[1], (STRATA, PIXELS, DB), 0, 5) < 3).astype(jnp.int32), jax.random.fold_in(part_keys[1], 1), 0, 1)
    pixel_factors = normal_values(part_keys[2], (PIXELS, RANK), 0.25, 1.5, ((0, 16),), jnp.float32)
    date_factors = normal_values(part_keys[3], (DATES, RANK), 0.25, 1.5, ((0, 16),), jnp.float32)
    return {"readings": readings, "coverage": coverage, "pixel_factors": pixel_factors, "date_factors": date_factors}


step_size = 0.05
ridge = 0.1
epsilon = 1e-06

def reference(readings, coverage, pixel_factors, date_factors):
    strips = pixel_factors.reshape(N_BLK, GP, RANK)
    blocks = date_factors.reshape(N_BLK, DB, RANK)
    hp = lax.Precision.HIGHEST
    for stratum in range(STRATA):
        values = readings[stratum].reshape(N_BLK, GP, DB)
        weights = coverage[stratum].reshape(N_BLK, GP, DB).astype(jnp.float32)
        predicted = jnp.einsum('gpr,gdr->gpd', strips, blocks, precision=hp)
        errors = weights * (values - predicted)
        pixel_grad = -jnp.einsum('gpd,gdr->gpr', errors, blocks, precision=hp) + ridge * strips
        date_grad = -jnp.einsum('gpd,gpr->gdr', errors, strips, precision=hp) + ridge * blocks
        pixel_ms = lax.optimization_barrier(jnp.sum(pixel_grad * pixel_grad, axis=(1, 2), keepdims=True)) / (GP * RANK)
        date_ms = lax.optimization_barrier(jnp.sum(date_grad * date_grad, axis=(1, 2), keepdims=True)) / (DB * RANK)
        strips = strips - step_size * pixel_grad / jnp.sqrt(pixel_ms + epsilon)
        blocks = blocks - step_size * date_grad / jnp.sqrt(date_ms + epsilon)
        blocks = jnp.roll(blocks, 1, axis=0)
    return (strips.reshape(PIXELS, RANK), blocks.reshape(DATES, RANK))
```

```python
import functools

import jax
import jax.numpy as jnp
from jax import lax
from jax.experimental import pallas as pl
from jax.experimental.pallas import tpu as pltpu
from jax.sharding import PartitionSpec as P

STRATA = 2
MESH = pl.DeviceIdType.MESH

step_size = 0.05
ridge = 0.1
epsilon = 1e-06

F32 = jnp.float32
BF16 = jnp.bfloat16


def split(value):
    high = value.astype(BF16)
    return high, (value - high.astype(F32)).astype(BF16)


def dot3(a, b, dims=((1,), (0,))):
    dot = functools.partial(
        lax.dot_general, dimension_numbers=(dims, ((), ())), preferred_element_type=F32
    )
    return dot(a[0], b[0]) + (dot(a[0], b[1]) + dot(a[1], b[0]))


def folded_squares(value):
    rows, columns = value.shape
    squares = value * value
    total = jnp.sum(squares.reshape(rows // 8, 8, columns), axis=0)
    return sum(total[:, i : i + 128] for i in range(0, columns, 128))


def whole_sum(value):
    return jnp.sum(jnp.sum(value, axis=0, keepdims=True), axis=1, keepdims=True)


def kernel(
    strips, groups, pieces, x_hbm, m_hbm, w_hbm, h_hbm, w_out, h_out,
    xs, ms, w, gw, wh, wl, eh, el, th, tl,
    h0, hprev, h1, hh, hl, gath, part, arecv, bsend, brecv, red, crecv, hrecv,
    psq, precv, dsq, drecv, wres, hres,
    lsem, ssem, rsem,
):
    z, s = lax.axis_index("blk"), lax.axis_index("sub")
    chips = groups // 2
    x, c = lax.div(s, 2), lax.rem(s, 2)
    rows, rank = w.shape
    share_rows = h_hbm.shape[0]
    piece = share_rows // pieces
    tile = 256 if rows % 256 == 0 else rows
    tiles = rows // tile
    znext, zprev = lax.rem(z + 1, strips), lax.rem(z + strips - 1, strips)
    mate = {"blk": z, "sub": 2 * x + 1 - c}
    ahead = {"blk": znext, "sub": s}
    pixel_count = rows * groups * rank
    date_count = share_rows * groups * rank

    def chip(step):
        return lax.rem(x + step + chips, chips)

    def cut(k):
        return pl.ds(k * piece, piece)

    used = [0]
    sent = []

    def slots(n):
        first = used[0]
        used[0] += n
        return first

    def send(src, dst, slot, device):
        copy = pltpu.make_async_remote_copy(
            src_ref=src, dst_ref=dst, send_sem=ssem.at[slot], recv_sem=rsem.at[slot],
            device_id=device, device_id_type=MESH,
        )
        copy.start()
        sent.append(copy)

    def arrived(dst, slot):
        pltpu.make_async_remote_copy(
            src_ref=dst, dst_ref=dst, send_sem=ssem.at[slot], recv_sem=rsem.at[slot],
            device_id=mate, device_id_type=MESH,
        ).wait_recv()

    loads = [
        pltpu.make_async_copy(h_hbm, h0.at[s], lsem.at[0]),
        pltpu.make_async_copy(w_hbm, w, lsem.at[1]),
        pltpu.make_async_copy(x_hbm.at[0], xs.at[0], lsem.at[2]),
        pltpu.make_async_copy(m_hbm.at[0], ms.at[0], lsem.at[3]),
        pltpu.make_async_copy(x_hbm.at[1], xs.at[1], lsem.at[4]),
        pltpu.make_async_copy(m_hbm.at[1], ms.at[1], lsem.at[5]),
    ]
    for load in loads:
        load.start()

    barrier = pltpu.get_barrier_semaphore()
    for step in range(1, groups):
        pl.semaphore_signal(
            barrier, inc=1, device_id={"blk": z, "sub": lax.rem(s + step, groups)},
            device_id_type=MESH,
        )
    for step in range(groups):
        for where in (znext, zprev):
            pl.semaphore_signal(
                barrier, inc=1, device_id={"blk": where, "sub": lax.rem(s + step, groups)},
                device_id_type=MESH,
            )
    pl.semaphore_wait(barrier, 3 * groups - 1)

    ag_x = slots(chips * pieces)
    ag_mate = slots(1)
    ag_fwd = slots(chips * pieces)
    hp_z = slots(chips)
    hp_mate = slots(chips)
    a_slot = [slots(chips) for _ in range(STRATA)]
    b_slot = [slots(chips * pieces) for _ in range(STRATA)]
    p_slot = [slots(groups) for _ in range(STRATA)]
    c_slot = [slots(pieces) for _ in range(STRATA)]
    d_slot = slots(chips * pieces)
    e_slot = slots(chips * pieces)
    h1_slot = slots(1)
    q_slot = slots(groups)

    for k in range(pieces):
        for i in range(1, chips):
            send(
                h_hbm.at[cut(k)], h0.at[s, cut(k)], ag_x + i * pieces + k,
                {"blk": z, "sub": 2 * chip(i) + c},
            )
    send(h_hbm, h0.at[s], ag_mate, mate)
    loads[0].wait()
    loads[1].wait()
    for b in range(tiles):
        at = pl.ds(b * tile, tile)
        wh[at, :], wl[at, :] = split(w[at, :])
    for k in range(pieces):
        for i in range(1, chips):
            share = 2 * chip(-i) + c
            arrived(h0.at[share, cut(k)], ag_x + i * pieces + k)
            send(h0.at[share, cut(k)], h0.at[share, cut(k)], ag_fwd + i * pieces + k, mate)
    arrived(h0.at[2 * x + 1 - c], ag_mate)
    for i in range(chips):
        share = 2 * chip(i) + c
        send(h0.at[share], hprev.at[share], hp_z + i, ahead)
    for k in range(pieces):
        for i in range(1, chips):
            arrived(h0.at[2 * chip(-i) + 1 - c, cut(k)], ag_fwd + i * pieces + k)

    def errors(t, held):
        hh[...], hl[...] = split(held[...].reshape(groups * share_rows, rank))
        loads[2 + 2 * t].wait()
        loads[3 + 2 * t].wait()
        for b in range(tiles):
            at = pl.ds(b * tile, tile)
            predicted = dot3((wh[at, :], wl[at, :]), (hh[...], hl[...]), ((1,), (1,)))
            e = ms[t, at, :].astype(F32) * (xs[t, at, :] - predicted)
            eh[at, :], el[at, :] = split(e)
            th[:, at], tl[:, at] = split(e.T)

    def date_sums(t, held):
        for i in [*range(1, chips), 0]:
            to = chip(i)
            at = pl.ds(pl.multiple_of(to * 2 * share_rows, 2 * share_rows), 2 * share_rows)
            sums = dot3((th[at, :], tl[at, :]), (wh[...], wl[...]))
            part[t, pl.ds(2 * to, 2)] = -sums.reshape(2, share_rows, rank)
            send(part.at[t, 2 * to + 1 - c], arecv.at[t, to], a_slot[t] + i, mate)
        for i in [*range(1, chips), 0]:
            to = chip(i)
            arrived(arecv.at[t, to], a_slot[t] + i)
            if i:
                for k in range(pieces):
                    bsend[t, i, cut(k)] = part[t, 2 * to + c, cut(k)] + arecv[t, to, cut(k)]
                    send(
                        bsend.at[t, i, cut(k)], brecv.at[t, i, cut(k)],
                        b_slot[t] + i * pieces + k, {"blk": z, "sub": 2 * to + c},
                    )
            else:
                red[t] = part[t, s] + arecv[t, to] + ridge * held[s]

    def pixel_grads(t):
        squares = jnp.zeros((8, 128), F32)
        for b in range(tiles):
            at = pl.ds(b * tile, tile)
            grad = ridge * w[at, :] - dot3((eh[at, :], el[at, :]), (hh[...], hl[...]))
            gw[at, :] = grad
            squares += folded_squares(grad)
        psq[t] = squares
        for step in range(1, groups):
            send(
                psq.at[t], precv.at[t, step], p_slot[t] + step,
                {"blk": z, "sub": lax.rem(s + step, groups)},
            )

    def date_shares(t, landing):
        for k in range(pieces):
            value = red[t, cut(k)]
            for i in range(1, chips):
                arrived(brecv.at[t, i, cut(k)], b_slot[t] + i * pieces + k)
                value += brecv[t, i, cut(k)]
            red[t, cut(k)] = value
            send(red.at[t, cut(k)], landing.at[cut(k)], c_slot[t] + k, ahead)

    def pixel_scale(t):
        total = psq[t]
        for step in range(1, groups):
            arrived(precv.at[t, step], p_slot[t] + step)
            total += precv[t, step]
        return step_size / jnp.sqrt(whole_sum(total) / pixel_count + epsilon)

    errors(0, h0)
    date_sums(0, h0)
    pixel_grads(0)
    date_shares(0, gath.at[s])
    for i in range(chips):
        share = 2 * chip(i) + c
        arrived(hprev.at[share], hp_z + i)
        send(hprev.at[share], hprev.at[share], hp_mate + i, mate)
    scale = pixel_scale(0)
    for b in range(tiles):
        at = pl.ds(b * tile, tile)
        value = w[at, :] - scale * gw[at, :]
        w[at, :] = value
        wh[at, :], wl[at, :] = split(value)

    for k in range(pieces):
        arrived(gath.at[s, cut(k)], c_slot[0] + k)
        for i in range(1, chips):
            send(
                gath.at[s, cut(k)], gath.at[s, cut(k)], d_slot + i * pieces + k,
                {"blk": z, "sub": 2 * chip(i) + c},
            )
        send(gath.at[s, cut(k)], gath.at[s, cut(k)], e_slot + k, mate)
    for k in range(pieces):
        for i in range(1, chips):
            share = 2 * chip(-i) + c
            arrived(gath.at[share, cut(k)], d_slot + i * pieces + k)
            send(gath.at[share, cut(k)], gath.at[share, cut(k)], e_slot + i * pieces + k, mate)
    for i in range(chips):
        arrived(hprev.at[2 * chip(i) + 1 - c], hp_mate + i)
    for k in range(pieces):
        for i in range(chips):
            arrived(gath.at[2 * chip(-i) + 1 - c, cut(k)], e_slot + i * pieces + k)
    grads = gath[...].reshape(groups * share_rows, rank)
    scale = step_size / jnp.sqrt(whole_sum(folded_squares(grads)) / date_count + epsilon)
    h1[...] = hprev[...] - scale.reshape(1, 1, 1) * gath[...]
    send(h1.at[s], hrecv, h1_slot, ahead)

    errors(1, h1)
    date_sums(1, h1)
    pixel_grads(1)
    date_shares(1, crecv)
    dsq[...] = folded_squares(red[1])
    for step in range(groups):
        send(
            dsq, drecv.at[step], q_slot + step,
            {"blk": znext, "sub": lax.rem(s + step, groups)},
        )
    scale = pixel_scale(1)
    for b in range(tiles):
        at = pl.ds(b * tile, tile)
        wres[at, :] = w[at, :] - scale * gw[at, :]
    w_store = pltpu.make_async_copy(wres, w_out, lsem.at[6])
    w_store.start()
    total = jnp.zeros((8, 128), F32)
    for step in range(groups):
        arrived(drecv.at[step], q_slot + step)
        total += drecv[step]
    scale = step_size / jnp.sqrt(whole_sum(total) / date_count + epsilon)
    arrived(hrecv, h1_slot)
    for k in range(pieces):
        arrived(crecv.at[cut(k)], c_slot[1] + k)
    hres[...] = hrecv[...] - scale * crecv[...]
    h_store = pltpu.make_async_copy(hres, h_out, lsem.at[7])
    h_store.start()
    for copy in sent:
        copy.wait_send()
    w_store.wait()
    h_store.wait()
    assert used[0] <= ssem.shape[0]


def on_device(strips, groups, readings, coverage, pixel_factors, date_factors):
    rows, rank = pixel_factors.shape
    share_rows = date_factors.shape[0]
    dates = share_rows * groups
    chips = groups // 2
    pieces = 2
    vmem = pltpu.VMEM
    block = vmem((groups, share_rows, rank), F32)
    by_chip = vmem((STRATA, chips, share_rows, rank), F32)
    share = vmem((share_rows, rank), F32)
    strip = vmem((rows, rank), F32)
    slots = 10 + 12 * chips * pieces + 12 * chips
    scratch = [
        vmem((STRATA, rows, dates), F32), vmem((STRATA, rows, dates), jnp.int32),
        strip, strip,
        vmem((rows, rank), BF16), vmem((rows, rank), BF16),
        vmem((rows, dates), BF16), vmem((rows, dates), BF16),
        vmem((dates, rows), BF16), vmem((dates, rows), BF16),
        block, block, block,
        vmem((dates, rank), BF16), vmem((dates, rank), BF16),
        block,
        vmem((STRATA, groups, share_rows, rank), F32),
        by_chip, by_chip, by_chip,
        vmem((STRATA, share_rows, rank), F32),
        share, share,
        vmem((STRATA, 8, 128), F32), vmem((STRATA, groups, 8, 128), F32),
        vmem((8, 128), F32), vmem((groups, 8, 128), F32),
        strip, share,
        pltpu.SemaphoreType.DMA((8,)),
        pltpu.SemaphoreType.DMA((slots,)),
        pltpu.SemaphoreType.DMA((slots,)),
    ]
    anywhere = pl.BlockSpec(memory_space=pl.ANY)
    return pl.pallas_call(
        functools.partial(kernel, strips, groups, pieces),
        out_shape=(
            jax.ShapeDtypeStruct((rows, rank), F32),
            jax.ShapeDtypeStruct((share_rows, rank), F32),
        ),
        in_specs=[pl.BlockSpec(memory_space=pltpu.HBM)] * 4,
        out_specs=(anywhere, anywhere),
        scratch_shapes=scratch,
        compiler_params=pltpu.CompilerParams(
            collective_id=0, has_side_effects=True, vmem_limit_bytes=48 * 1024 * 1024
        ),
    )(readings, coverage, pixel_factors, date_factors)


def solution(mesh):
    in_specs = (
        P(None, ("parts", "blk", "sub"), None),
        P(None, ("parts", "blk", "sub"), None),
        P(("parts", "blk", "sub"), None),
        P(("parts", "blk", "sub"), None),
    )
    out_specs = (P(("parts", "blk", "sub"), None), P(("parts", "blk", "sub"), None))
    return jax.shard_map(
        functools.partial(on_device, mesh.shape["blk"], mesh.shape["sub"]),
        mesh=mesh, in_specs=in_specs, out_specs=out_specs, check_vma=False,
    )
```

```python
import functools

import jax
import jax.numpy as jnp
from jax import lax
from jax.experimental import pallas as pl
from jax.experimental.pallas import tpu as pltpu
from jax.sharding import PartitionSpec as P

STRATA = 2
MESH = pl.DeviceIdType.MESH

step_size = 0.05
ridge = 0.1
epsilon = 1e-06

F32 = jnp.float32
BF16 = jnp.bfloat16


def split(value):
    high = value.astype(BF16)
    return high, (value - high.astype(F32)).astype(BF16)


def dot3(a, b, dims=((1,), (0,))):
    dot = functools.partial(
        lax.dot_general, dimension_numbers=(dims, ((), ())), preferred_element_type=F32
    )
    return dot(a[0], b[0]) + (dot(a[0], b[1]) + dot(a[1], b[0]))


def folded_squares(value):
    rows, columns = value.shape
    squares = value * value
    total = jnp.sum(squares.reshape(rows // 8, 8, columns), axis=0)
    return sum(total[:, i : i + 128] for i in range(0, columns, 128))


def whole_sum(value):
    return jnp.sum(jnp.sum(value, axis=0, keepdims=True), axis=1, keepdims=True)


def kernel(
    strips, groups, x_hbm, m_hbm, w_hbm, h_hbm, w_out, h_out,
    xs, ms, w, gw, wh, wl, eh, el, th, tl,
    h0, hprev, h1, hh, hl, gath, part, arecv, red, crecv, hrecv,
    psq, precv, dsq, drecv, wres, hres,
    lsem, ssem, rsem,
):
    z, s = lax.axis_index("blk"), lax.axis_index("sub")
    chips = groups // 2
    x, c = lax.div(s, 2), lax.rem(s, 2)
    rows, rank = w.shape
    share_rows = h_hbm.shape[0]
    tile = 256 if rows % 256 == 0 else rows
    tiles = rows // tile
    znext, zprev = lax.rem(z + 1, strips), lax.rem(z + strips - 1, strips)
    mate = {"blk": z, "sub": 2 * x + 1 - c}
    ahead = {"blk": znext, "sub": s}
    pixel_count = rows * groups * rank
    date_count = share_rows * groups * rank

    def chip(step):
        return lax.rem(x + step + chips, chips)

    def peer(step):
        return lax.rem(s + step + groups, groups)

    used = [0]
    sent = []

    def slots(n):
        first = used[0]
        used[0] += n
        return first

    def send(src, dst, slot, device):
        copy = pltpu.make_async_remote_copy(
            src_ref=src, dst_ref=dst, send_sem=ssem.at[slot], recv_sem=rsem.at[slot],
            device_id=device, device_id_type=MESH,
        )
        copy.start()
        sent.append(copy)

    def arrived(dst, slot):
        pltpu.make_async_remote_copy(
            src_ref=dst, dst_ref=dst, send_sem=ssem.at[slot], recv_sem=rsem.at[slot],
            device_id=mate, device_id_type=MESH,
        ).wait_recv()

    loads = [
        pltpu.make_async_copy(h_hbm, h0.at[s], lsem.at[0]),
        pltpu.make_async_copy(w_hbm, w, lsem.at[1]),
        pltpu.make_async_copy(x_hbm.at[0], xs.at[0], lsem.at[2]),
        pltpu.make_async_copy(m_hbm.at[0], ms.at[0], lsem.at[3]),
        pltpu.make_async_copy(x_hbm.at[1], xs.at[1], lsem.at[4]),
        pltpu.make_async_copy(m_hbm.at[1], ms.at[1], lsem.at[5]),
    ]
    for load in loads:
        load.start()

    barrier = pltpu.get_barrier_semaphore()
    for step in range(1, groups):
        pl.semaphore_signal(
            barrier, inc=1, device_id={"blk": z, "sub": peer(step)},
            device_id_type=MESH,
        )
    for step in range(groups):
        pl.semaphore_signal(
            barrier, inc=1, device_id={"blk": zprev, "sub": peer(step)}, device_id_type=MESH
        )
    loads[1].wait()
    for b in range(tiles):
        at = pl.ds(b * tile, tile)
        wh[at, :], wl[at, :] = split(w[at, :])
    loads[0].wait()
    pl.semaphore_wait(barrier, 2 * groups - 1)

    ag_slot = slots(groups)
    hp_slot = slots(1)
    a_slot = [slots(groups) for _ in range(STRATA)]
    p_slot = [slots(groups) for _ in range(STRATA)]
    c_slot = slots(groups)
    e_slot = slots(groups)
    last_slot = slots(1)
    h1_slot = slots(1)
    q_slot = slots(groups)

    for step in range(1, groups):
        send(h_hbm, h0.at[s], ag_slot + step, {"blk": z, "sub": peer(step)})
    for step in range(1, groups):
        arrived(h0.at[peer(-step)], ag_slot + step)
    send(h0, hprev, hp_slot, ahead)

    def errors(t, held):
        hh[...], hl[...] = split(held[...].reshape(groups * share_rows, rank))
        loads[2 + 2 * t].wait()
        loads[3 + 2 * t].wait()
        for b in range(tiles):
            at = pl.ds(b * tile, tile)
            predicted = dot3((wh[at, :], wl[at, :]), (hh[...], hl[...]), ((1,), (1,)))
            e = ms[t, at, :].astype(F32) * (xs[t, at, :] - predicted)
            eh[at, :], el[at, :] = split(e)
            th[:, at], tl[:, at] = split(e.T)

    def date_sums(t):
        sums = dot3((th[...], tl[...]), (wh[...], wl[...]))
        part[t] = -sums.reshape(groups, share_rows, rank)
        for step in range(1, groups):
            send(
                part.at[t, peer(step)], arecv.at[t, step], a_slot[t] + step,
                {"blk": z, "sub": peer(step)},
            )

    def pixel_grads(t):
        squares = jnp.zeros((8, 128), F32)
        for b in range(tiles):
            at = pl.ds(b * tile, tile)
            grad = ridge * w[at, :] - dot3((eh[at, :], el[at, :]), (hh[...], hl[...]))
            gw[at, :] = grad
            squares += folded_squares(grad)
        psq[t] = squares
        for step in range(1, groups):
            send(
                psq.at[t], precv.at[t, step], p_slot[t] + step,
                {"blk": z, "sub": peer(step)},
            )

    def date_share(t, held):
        value = part[t, s] + ridge * held[s]
        for step in range(1, groups):
            arrived(arecv.at[t, step], a_slot[t] + step)
            value += arecv[t, step]
        red[t] = value

    def pixel_scale(t):
        total = psq[t]
        for step in range(1, groups):
            arrived(precv.at[t, step], p_slot[t] + step)
            total += precv[t, step]
        return step_size / jnp.sqrt(whole_sum(total) / pixel_count + epsilon)

    errors(0, h0)
    date_sums(0)
    pixel_grads(0)
    date_share(0, h0)
    for i in range(chips):
        send(
            red.at[0], gath.at[s], c_slot + i, {"blk": znext, "sub": 2 * chip(i) + c}
        )
    scale = pixel_scale(0)
    for b in range(tiles):
        at = pl.ds(b * tile, tile)
        value = w[at, :] - scale * gw[at, :]
        w[at, :] = value
        wh[at, :], wl[at, :] = split(value)

    for i in range(chips):
        share = 2 * chip(-i) + c
        arrived(gath.at[share], c_slot + i)
        send(gath.at[share], gath.at[share], e_slot + i, mate)
    for i in range(chips):
        arrived(gath.at[2 * chip(-i) + 1 - c], e_slot + i)
    arrived(hprev, hp_slot)
    grads = gath[...].reshape(groups * share_rows, rank)
    scale = step_size / jnp.sqrt(whole_sum(folded_squares(grads)) / date_count + epsilon)
    h1[...] = hprev[...] - scale.reshape(1, 1, 1) * gath[...]
    send(h1.at[s], hrecv, h1_slot, ahead)

    errors(1, h1)
    date_sums(1)
    pixel_grads(1)
    date_share(1, h1)
    send(red.at[1], crecv, last_slot, ahead)
    dsq[...] = folded_squares(red[1])
    for step in range(groups):
        send(
            dsq, drecv.at[step], q_slot + step,
            {"blk": znext, "sub": peer(step)},
        )
    scale = pixel_scale(1)
    for b in range(tiles):
        at = pl.ds(b * tile, tile)
        wres[at, :] = w[at, :] - scale * gw[at, :]
    w_store = pltpu.make_async_copy(wres, w_out, lsem.at[6])
    w_store.start()
    total = jnp.zeros((8, 128), F32)
    for step in range(groups):
        arrived(drecv.at[step], q_slot + step)
        total += drecv[step]
    scale = step_size / jnp.sqrt(whole_sum(total) / date_count + epsilon)
    arrived(hrecv, h1_slot)
    arrived(crecv, last_slot)
    hres[...] = hrecv[...] - scale * crecv[...]
    h_store = pltpu.make_async_copy(hres, h_out, lsem.at[7])
    h_store.start()
    for copy in sent:
        copy.wait_send()
    w_store.wait()
    h_store.wait()
    assert used[0] <= ssem.shape[0]


def on_device(strips, groups, readings, coverage, pixel_factors, date_factors):
    rows, rank = pixel_factors.shape
    share_rows = date_factors.shape[0]
    dates = share_rows * groups
    vmem = pltpu.VMEM
    block = vmem((groups, share_rows, rank), F32)
    share = vmem((share_rows, rank), F32)
    strip = vmem((rows, rank), F32)
    slots = 8 + 9 * groups
    scratch = [
        vmem((STRATA, rows, dates), F32), vmem((STRATA, rows, dates), jnp.int32),
        strip, strip,
        vmem((rows, rank), BF16), vmem((rows, rank), BF16),
        vmem((rows, dates), BF16), vmem((rows, dates), BF16),
        vmem((dates, rows), BF16), vmem((dates, rows), BF16),
        block, block, block,
        vmem((dates, rank), BF16), vmem((dates, rank), BF16),
        block,
        vmem((STRATA, groups, share_rows, rank), F32),
        vmem((STRATA, groups, share_rows, rank), F32),
        vmem((STRATA, share_rows, rank), F32),
        share, share,
        vmem((STRATA, 8, 128), F32), vmem((STRATA, groups, 8, 128), F32),
        vmem((8, 128), F32), vmem((groups, 8, 128), F32),
        strip, share,
        pltpu.SemaphoreType.DMA((8,)),
        pltpu.SemaphoreType.DMA((slots,)),
        pltpu.SemaphoreType.DMA((slots,)),
    ]
    anywhere = pl.BlockSpec(memory_space=pl.ANY)
    return pl.pallas_call(
        functools.partial(kernel, strips, groups),
        out_shape=(
            jax.ShapeDtypeStruct((rows, rank), F32),
            jax.ShapeDtypeStruct((share_rows, rank), F32),
        ),
        in_specs=[pl.BlockSpec(memory_space=pltpu.HBM)] * 4,
        out_specs=(anywhere, anywhere),
        scratch_shapes=scratch,
        compiler_params=pltpu.CompilerParams(
            collective_id=0, has_side_effects=True, vmem_limit_bytes=53 * 1024 * 1024
        ),
    )(readings, coverage, pixel_factors, date_factors)


def solution(mesh):
    in_specs = (
        P(None, ("parts", "blk", "sub"), None),
        P(None, ("parts", "blk", "sub"), None),
        P(("parts", "blk", "sub"), None),
        P(("parts", "blk", "sub"), None),
    )
    out_specs = (P(("parts", "blk", "sub"), None), P(("parts", "blk", "sub"), None))
    return jax.shard_map(
        functools.partial(on_device, mesh.shape["blk"], mesh.shape["sub"]),
        mesh=mesh, in_specs=in_specs, out_specs=out_specs, check_vma=False,
    )
```

```python
import functools

import jax
import jax.numpy as jnp
from jax import lax
from jax.experimental import pallas as pl
from jax.experimental.pallas import tpu as pltpu
from jax.sharding import PartitionSpec as P

STRATA = 2
MESH = pl.DeviceIdType.MESH

step_size = 0.05
ridge = 0.1
epsilon = 1e-06

F32 = jnp.float32
BF16 = jnp.bfloat16


def split(value):
    high = value.astype(BF16)
    return high, (value - high.astype(F32)).astype(BF16)


def dot3(a, b, dims=((1,), (0,))):
    dot = functools.partial(
        lax.dot_general, dimension_numbers=(dims, ((), ())), preferred_element_type=F32
    )
    return dot(a[0], b[0]) + (dot(a[0], b[1]) + dot(a[1], b[0]))


def folded_squares(value):
    rows, columns = value.shape
    squares = value * value
    total = jnp.sum(squares.reshape(rows // 8, 8, columns), axis=0)
    return sum(total[:, i : i + 128] for i in range(0, columns, 128))


def whole_sum(value):
    return jnp.sum(jnp.sum(value, axis=0, keepdims=True), axis=1, keepdims=True)


def kernel(
    strips, groups, x_hbm, m_hbm, w_hbm, h_hbm, w_out, h_out,
    xs, ms, w, gw, wh, wl, eh, el, th, tl,
    h0, hprev, h1, hh, hl, gath, part, arecv, red, crecv, hrecv,
    psq, precv, dsq, drecv, wres, hres,
    lsem, ssem, rsem,
):
    z, s = lax.axis_index("blk"), lax.axis_index("sub")
    chips = groups // 2
    x, c = lax.div(s, 2), lax.rem(s, 2)
    rows, rank = w.shape
    share_rows = h_hbm.shape[0]
    tile = 256 if rows % 256 == 0 else rows
    tiles = rows // tile
    znext, zprev = lax.rem(z + 1, strips), lax.rem(z + strips - 1, strips)
    mate = {"blk": z, "sub": 2 * x + 1 - c}
    ahead = {"blk": znext, "sub": s}
    pixel_count = rows * groups * rank
    date_count = share_rows * groups * rank

    def chip(step):
        return lax.rem(x + step + chips, chips)

    def peer(step):
        return lax.rem(s + step + groups, groups)

    used = [0]
    sent = []

    def slots(n):
        first = used[0]
        used[0] += n
        return first

    def send(src, dst, slot, device):
        copy = pltpu.make_async_remote_copy(
            src_ref=src, dst_ref=dst, send_sem=ssem.at[slot], recv_sem=rsem.at[slot],
            device_id=device, device_id_type=MESH,
        )
        copy.start()
        sent.append(copy)

    def arrived(dst, slot):
        pltpu.make_async_remote_copy(
            src_ref=dst, dst_ref=dst, send_sem=ssem.at[slot], recv_sem=rsem.at[slot],
            device_id=mate, device_id_type=MESH,
        ).wait_recv()

    loads = [
        pltpu.make_async_copy(h_hbm, h0.at[s], lsem.at[0]),
        pltpu.make_async_copy(w_hbm, w, lsem.at[1]),
        pltpu.make_async_copy(x_hbm.at[0], xs.at[0], lsem.at[2]),
        pltpu.make_async_copy(m_hbm.at[0], ms.at[0], lsem.at[3]),
        pltpu.make_async_copy(x_hbm.at[1], xs.at[1], lsem.at[4]),
        pltpu.make_async_copy(m_hbm.at[1], ms.at[1], lsem.at[5]),
    ]
    for load in loads:
        load.start()

    barrier = pltpu.get_barrier_semaphore()
    for step in range(1, groups):
        pl.semaphore_signal(
            barrier, inc=1, device_id={"blk": z, "sub": peer(step)},
            device_id_type=MESH,
        )
    for step in range(groups):
        pl.semaphore_signal(
            barrier, inc=1, device_id={"blk": zprev, "sub": peer(step)}, device_id_type=MESH
        )
    loads[1].wait()
    for b in range(tiles):
        at = pl.ds(b * tile, tile)
        wh[at, :], wl[at, :] = split(w[at, :])
    loads[0].wait()
    pl.semaphore_wait(barrier, 2 * groups - 1)

    ag_slot = slots(groups)
    hp_slot = slots(1)
    a_slot = [slots(groups) for _ in range(STRATA)]
    p_slot = [slots(groups) for _ in range(STRATA)]
    c_slot = slots(groups)
    e_slot = slots(groups)
    last_slot = slots(1)
    h1_slot = slots(1)
    q_slot = slots(groups)

    for step in range(1, groups):
        send(h_hbm, h0.at[s], ag_slot + step, {"blk": z, "sub": peer(step)})
    for step in range(1, groups):
        arrived(h0.at[peer(-step)], ag_slot + step)
    send(h0, hprev, hp_slot, ahead)

    def errors(t, held):
        hh[...], hl[...] = split(held[...].reshape(groups * share_rows, rank))
        loads[2 + 2 * t].wait()
        loads[3 + 2 * t].wait()
        for b in range(tiles):
            at = pl.ds(b * tile, tile)
            predicted = dot3((wh[at, :], wl[at, :]), (hh[...], hl[...]), ((1,), (1,)))
            e = ms[t, at, :].astype(F32) * (xs[t, at, :] - predicted)
            eh[at, :], el[at, :] = split(e)
            th[:, at], tl[:, at] = split(e.T)

    def date_sums(t):
        sums = dot3((th[...], tl[...]), (wh[...], wl[...]))
        part[t] = -sums.reshape(groups, share_rows, rank)
        for step in range(1, groups):
            send(
                part.at[t, peer(step)], arecv.at[t, step], a_slot[t] + step,
                {"blk": z, "sub": peer(step)},
            )

    def pixel_grads(t):
        squares = jnp.zeros((8, 128), F32)
        for b in range(tiles):
            at = pl.ds(b * tile, tile)
            grad = ridge * w[at, :] - dot3((eh[at, :], el[at, :]), (hh[...], hl[...]))
            gw[at, :] = grad
            squares += folded_squares(grad)
        psq[t] = squares
        for step in range(1, groups):
            send(
                psq.at[t], precv.at[t, step], p_slot[t] + step,
                {"blk": z, "sub": peer(step)},
            )

    def date_share(t, held):
        value = part[t, s] + ridge * held[s]
        for step in range(1, groups):
            arrived(arecv.at[t, step], a_slot[t] + step)
            value += arecv[t, step]
        red[t] = value

    def pixel_scale(t):
        total = psq[t]
        for step in range(1, groups):
            arrived(precv.at[t, step], p_slot[t] + step)
            total += precv[t, step]
        return step_size / jnp.sqrt(whole_sum(total) / pixel_count + epsilon)

    errors(0, h0)
    date_sums(0)
    pixel_grads(0)
    date_share(0, h0)
    for i in range(chips):
        send(
            red.at[0], gath.at[s], c_slot + i, {"blk": znext, "sub": 2 * chip(i) + c}
        )
    scale = pixel_scale(0)
    for b in range(tiles):
        at = pl.ds(b * tile, tile)
        value = w[at, :] - scale * gw[at, :]
        w[at, :] = value
        wh[at, :], wl[at, :] = split(value)

    for i in range(chips):
        share = 2 * chip(-i) + c
        arrived(gath.at[share], c_slot + i)
        send(gath.at[share], gath.at[share], e_slot + i, mate)
    for i in range(chips):
        arrived(gath.at[2 * chip(-i) + 1 - c], e_slot + i)
    arrived(hprev, hp_slot)
    grads = gath[...].reshape(groups * share_rows, rank)
    scale = step_size / jnp.sqrt(whole_sum(folded_squares(grads)) / date_count + epsilon)
    h1[...] = hprev[...] - scale.reshape(1, 1, 1) * gath[...]
    send(h1.at[s], hrecv, h1_slot, ahead)

    errors(1, h1)
    date_sums(1)
    pixel_grads(1)
    date_share(1, h1)
    send(red.at[1], crecv, last_slot, ahead)
    dsq[...] = folded_squares(red[1])
    for step in range(groups):
        send(
            dsq, drecv.at[step], q_slot + step,
            {"blk": znext, "sub": peer(step)},
        )
    scale = pixel_scale(1)
    for b in range(tiles):
        at = pl.ds(b * tile, tile)
        wres[at, :] = w[at, :] - scale * gw[at, :]
    w_store = pltpu.make_async_copy(wres, w_out, lsem.at[6])
    w_store.start()
    total = jnp.zeros((8, 128), F32)
    for step in range(groups):
        arrived(drecv.at[step], q_slot + step)
        total += drecv[step]
    scale = step_size / jnp.sqrt(whole_sum(total) / date_count + epsilon)
    arrived(hrecv, h1_slot)
    arrived(crecv, last_slot)
    hres[...] = hrecv[...] - scale * crecv[...]
    h_store = pltpu.make_async_copy(hres, h_out, lsem.at[7])
    h_store.start()
    for copy in sent:
        copy.wait_send()
    w_store.wait()
    h_store.wait()
    assert used[0] <= ssem.shape[0]


def hand_on(w_from, h_from, w_out, h_out, sem):
    copies = [
        pltpu.make_async_copy(w_from, w_out, sem.at[0]),
        pltpu.make_async_copy(h_from, h_out, sem.at[1]),
    ]
    for copy in copies:
        copy.start()
    for copy in copies:
        copy.wait()


def on_device(strips, groups, readings, coverage, pixel_factors, date_factors):
    rows, rank = pixel_factors.shape
    share_rows = date_factors.shape[0]
    dates = share_rows * groups
    vmem = pltpu.VMEM
    block = vmem((groups, share_rows, rank), F32)
    share = vmem((share_rows, rank), F32)
    strip = vmem((rows, rank), F32)
    slots = 8 + 9 * groups
    scratch = [
        vmem((STRATA, rows, dates), F32), vmem((STRATA, rows, dates), jnp.int32),
        strip, strip,
        vmem((rows, rank), BF16), vmem((rows, rank), BF16),
        vmem((rows, dates), BF16), vmem((rows, dates), BF16),
        vmem((dates, rows), BF16), vmem((dates, rows), BF16),
        block, block, block,
        vmem((dates, rank), BF16), vmem((dates, rank), BF16),
        block,
        vmem((STRATA, groups, share_rows, rank), F32),
        vmem((STRATA, groups, share_rows, rank), F32),
        vmem((STRATA, share_rows, rank), F32),
        share, share,
        vmem((STRATA, 8, 128), F32), vmem((STRATA, groups, 8, 128), F32),
        vmem((8, 128), F32), vmem((groups, 8, 128), F32),
        strip, share,
        pltpu.SemaphoreType.DMA((8,)),
        pltpu.SemaphoreType.DMA((slots,)),
        pltpu.SemaphoreType.DMA((slots,)),
    ]
    anywhere = pl.BlockSpec(memory_space=pl.ANY)
    strip_value, share_value = pl.pallas_call(
        functools.partial(kernel, strips, groups),
        out_shape=(
            jax.ShapeDtypeStruct((rows, rank), F32),
            jax.ShapeDtypeStruct((share_rows, rank), F32),
        ),
        in_specs=[pl.BlockSpec(memory_space=pltpu.HBM)] * 4,
        out_specs=(anywhere, anywhere),
        scratch_shapes=scratch,
        compiler_params=pltpu.CompilerParams(
            collective_id=0, has_side_effects=True, vmem_limit_bytes=53 * 1024 * 1024
        ),
    )(readings, coverage, pixel_factors, date_factors)
    return pl.pallas_call(
        hand_on,
        out_shape=(
            jax.ShapeDtypeStruct((rows, rank), F32),
            jax.ShapeDtypeStruct((share_rows, rank), F32),
        ),
        in_specs=[pl.BlockSpec(memory_space=pltpu.VMEM)] * 2,
        out_specs=(anywhere, anywhere),
        scratch_shapes=[pltpu.SemaphoreType.DMA((2,))],
        compiler_params=pltpu.CompilerParams(vmem_limit_bytes=8 * 1024 * 1024),
    )(strip_value, share_value)


def solution(mesh):
    in_specs = (
        P(None, ("parts", "blk", "sub"), None),
        P(None, ("parts", "blk", "sub"), None),
        P(("parts", "blk", "sub"), None),
        P(("parts", "blk", "sub"), None),
    )
    out_specs = (P(("parts", "blk", "sub"), None), P(("parts", "blk", "sub"), None))
    return jax.shard_map(
        functools.partial(on_device, mesh.shape["blk"], mesh.shape["sub"]),
        mesh=mesh, in_specs=in_specs, out_specs=out_specs, check_vma=False,
    )
```
